32 devices in a mesh: fsdp: 4 (over x, core), ctx: 2 (over y), tp: 4 (over z).
Axes of the slice: x: 2, y: 2, z: 4, core: 2. Of those that a mesh axis runs over, the one named last changes fastest.
Arguments:
- tokens: bfloat16 [4, 1280, 768], P('fsdp', 'ctx'), may hold values from -6 to 6
- counts: int32 [4, 2], P('fsdp'), may hold values from 1 to 640, as said below
- qkv_weight: bfloat16 [2, 3, 768, 768], P(None, None, ('fsdp', 'ctx'), 'tp'), may hold values from -0.3125 to 0.3125
- qv_bias: float32 [2, 2, 768], P(None, None, 'tp'), may hold values from -3 to 3
- out_weight: bfloat16 [2, 768, 768], P(None, 'tp', ('fsdp', 'ctx')), may hold values from -1.25 to 1.25
- out_bias: float32 [2, 768], replicated, may hold values from -3 to 3
- norm_gain: float32 [2, 2, 768], replicated, may hold values from 0.5 to 1.5
- norm_bias: float32 [2, 2, 768], replicated, may hold values from -2 to 2
- up_weight: bfloat16 [2, 768, 3072], P(None, ('fsdp', 'ctx'), 'tp'), may hold values from -0.21875 to 0.21875
- up_bias: float32 [2, 3072], P(None, 'tp'), may hold values from -3 to 3
- down_weight: bfloat16 [2, 3072, 768], P(None, 'tp', ('fsdp', 'ctx')), may hold values from -0.109375 to 0.109375
- down_bias: float32 [2, 768], replicated, may hold values from -3 to 3
- cotangent: bfloat16 [4, 1280, 768], P('fsdp', 'ctx'), may hold values from -6 to 6
Outputs:
- block_output: bfloat16 [4, 1280, 768], P('fsdp', 'ctx')
- grad_tokens: float32 [4, 1280, 768], P('fsdp', 'ctx')
- grad_qkv_weight: float32 [2, 3, 768, 768], P(None, None, ('fsdp', 'ctx'), 'tp')
- grad_qv_bias: float32 [2, 2, 768], P(None, None, 'tp')
- grad_out_weight: float32 [2, 768, 768], P(None, 'tp', ('fsdp', 'ctx'))
- grad_out_bias: float32 [2, 768], replicated
- grad_norm_gain: float32 [2, 2, 768], replicated
- grad_norm_bias: float32 [2, 2, 768], replicated
- grad_up_weight: float32 [2, 768, 3072], P(None, ('fsdp', 'ctx'), 'tp')
- grad_up_bias: float32 [2, 3072], P(None, 'tp')
- grad_down_weight: float32 [2, 3072, 768], P(None, 'tp', ('fsdp', 'ctx'))
- grad_down_bias: float32 [2, 768], replicated
The draws below stay inside these ranges and needn't reach their ends.
Inputs may be any that keep to these rules, and one draw needn't show every extreme that they name: counts[i, c] is the number of live rows of block c of image i; each row of counts sums to 1024 and has 640 as its largest entry.
All inputs are finite; a program needn't handle non-finite values.
Results may differ from the reference program's by a relative error of at most 0.025.
The reference program's roundings to bfloat16 on the way count: a program that leaves them out, or rounds other values in their place, can miss the bound.
Values may be sent and summed in bfloat16 or wider, within the bound.
A program may use at most 192 MiB of HBM per device.

```python
import math
import jax
import jax.numpy as jnp
from jax import lax

D = 768
HEADS = 12
HD = 64
FF = 3072
LAYERS = 2
SEQ = 1024
CAP = 640
IMAGES = 4
N_CTX = 2


def counts_row_draw(key):
    key_full, key_moves = jax.random.split(key)
    others = N_CTX - 1
    rest = SEQ - CAP
    full_at = jax.random.randint(key_full, (), 0, N_CTX)
    if others == 0:
        return jnp.full((1,), CAP, jnp.int32)
    base = rest // others
    extra = rest - base * others
    lanes = jnp.arange(others, dtype=jnp.int32)
    filled = (base + (lanes < extra).astype(jnp.int32)).astype(jnp.int32)

    def move(step_no, values):
        step_key = jax.random.fold_in(key_moves, step_no)
        key_a, key_b, key_c = jax.random.split(step_key, 3)
        source = jax.random.randint(key_a, (), 0, others)
        target = jax.random.randint(key_b, (), 0, others)
        room = jnp.minimum(values[source] - 1, CAP - values[target])
        room = jnp.where(source == target, 0, jnp.maximum(room, 0))
        amount = jax.random.randint(key_c, (), 0, room + 1)
        values = values.at[source].add(-amount)
        return values.at[target].add(amount)
    filled = lax.fori_loop(0, 4 * others + 4, move, filled)
    columns = jnp.arange(N_CTX, dtype=jnp.int32)
    pick = jnp.clip(columns - (columns > full_at).astype(jnp.int32), 0, others - 1)
    return jnp.where(columns == full_at, CAP, filled[pick]).astype(jnp.int32)


def draw_counts(key, part):
    key = jax.random.fold_in(key, 11)
    keys = jax.random.split(key, IMAGES)
    return jax.vmap(counts_row_draw)(keys).astype(jnp.int32)


def shard_levels(key, shape, pieces, low, largest):
    loudness = 1.0
    for dim, blocks in pieces:
        draws = jax.random.uniform(jax.random.fold_in(jax.random.fold_in(key, 6), dim), (blocks,), jnp.float32, low / len(pieces), largest / len(pieces))
        loudness = loudness * jnp.repeat(jnp.exp(draws), shape[dim] // blocks).reshape((-1,) + (1,) * (len(shape) - 1 - dim))
    return loudness


def bell_draw(own_key, extent, deviation, reach, cuts=(), held_as=jnp.bfloat16):
    values = jax.random.normal(own_key, extent, jnp.float32) * deviation
    if len(cuts) > 0:
        values = shard_levels(own_key, extent, cuts, -0.22, 0.18) * values
    return jnp.clip(values, min=-reach, max=reach).astype(held_as)


def setup_inputs(seed: int = 0) -> dict:
    arg_keys = jax.random.split(jax.random.key(seed), 14)
    return {
        "tokens": bell_draw(arg_keys[0], (IMAGES, N_CTX * CAP, D), 1.0, 6.0, ((0, 4), (1, 2))),
        "counts": draw_counts(jax.random.fold_in(arg_keys[13], 71), 0),
        "qkv_weight": bell_draw(arg_keys[2], (LAYERS, 3, D, D), (D // 2) ** -0.5, 0.3125, ((2, 8), (3, 4))),
        "qv_bias": bell_draw(arg_keys[3], (LAYERS, 2, D), 0.5, 3.0, ((2, 4),), jnp.float32),
        "out_weight": bell_draw(arg_keys[4], (LAYERS, D, D), (D // 32) ** -0.5, 1.25, ((1, 4), (2, 8))),
        "out_bias": bell_draw(arg_keys[5], (LAYERS, D), 0.5, 3.0, (), jnp.float32),
        "norm_gain": jnp.clip(1.0 + 0.1 * jax.random.normal(arg_keys[6], (LAYERS, 2, D), jnp.float32), 0.5, 1.5),
        "norm_bias": bell_draw(arg_keys[7], (LAYERS, 2, D), 0.3, 2.0, (), jnp.float32),
        "up_weight": bell_draw(arg_keys[8], (LAYERS, D, FF), D ** -0.5, 0.21875, ((1, 8), (2, 4))),
        "up_bias": bell_draw(arg_keys[9], (LAYERS, FF), 0.5, 3.0, ((1, 4),), jnp.float32),
        "down_weight": bell_draw(arg_keys[10], (LAYERS, FF, D), FF ** -0.5, 0.109375, ((1, 4), (2, 8))),
        "down_bias": bell_draw(arg_keys[11], (LAYERS, D), 0.5, 3.0, (), jnp.float32),
        "cotangent": bell_draw(arg_keys[12], (IMAGES, N_CTX * CAP, D), 1.0, 6.0, ((0, 4), (1, 2))),
    }


@jax.custom_vjp
def low(v):
    return lax.optimization_barrier(v.astype(jnp.bfloat16)).astype(jnp.float32)

@jax.custom_vjp
def low_back(v):
    return v

def low_keep(v):
    return (low(v), None)

def low_pass(kept, grad):
    return (grad,)

def back_keep(v):
    return (v, None)

def back_low(kept, grad):
    return (low(grad),)
low.defvjp(low_keep, low_pass)
low_back.defvjp(back_keep, back_low)
norm_eps = 1e-06
highest = lax.Precision.HIGHEST

def rounded(value):
    return low(low_back(value))

def layer_norm(values, norm_scale, norm_shift):
    centred = values - lax.optimization_barrier(jnp.mean(values, -1, keepdims=True))
    inverse = lax.rsqrt(lax.optimization_barrier(jnp.mean(centred * centred, -1, keepdims=True)) + norm_eps)
    return centred * inverse * norm_scale + norm_shift

def attend(queries, keys_all, values_all):
    block_rows = math.gcd(SEQ, 512)
    blocks = queries.reshape(SEQ // block_rows, block_rows, HEADS, HD)

    def one_block(query_block):
        scores = low_back(jnp.einsum('qhd,khd->hqk', query_block, keys_all, precision=highest) * HD ** (-0.5))
        weights = jax.nn.softmax(scores, axis=-1)
        return jnp.einsum('hqk,khd->qhd', weights, values_all, precision=highest)
    return lax.map(jax.checkpoint(one_block), blocks).reshape(SEQ, HEADS * HD)

def forward(stream, qkv_weight, qv_bias, out_weight, out_bias, norm_gain, norm_bias, up_weight, up_bias, down_weight, down_bias):
    head_shape = (IMAGES, SEQ, HEADS, HD)
    for layer_no in range(LAYERS):
        normed = low(layer_norm(stream, norm_gain[layer_no, 0], norm_bias[layer_no, 0]))
        project = jnp.einsum('isd,kde->kise', normed, qkv_weight[layer_no], precision=highest)
        query = rounded(project[0] + qv_bias[layer_no, 0])
        key_proj = rounded(project[1])
        value_proj = rounded(project[2] + qv_bias[layer_no, 1])
        attended = jax.vmap(attend)(query.reshape(head_shape), key_proj.reshape(head_shape), value_proj.reshape(head_shape))
        attended = rounded(attended)
        mixed = low_back(jnp.einsum('isd,de->ise', attended, out_weight[layer_no], precision=highest) + out_bias[layer_no])
        hidden = stream + mixed
        normed_two = low(layer_norm(hidden, norm_gain[layer_no, 1], norm_bias[layer_no, 1]))
        pre_act = low_back(jnp.einsum('isd,df->isf', normed_two, up_weight[layer_no], precision=highest) + up_bias[layer_no])
        activated = low(jax.nn.gelu(pre_act, approximate=False))
        branch = low_back(jnp.einsum('isf,fd->isd', activated, down_weight[layer_no], precision=highest) + down_bias[layer_no])
        stream = hidden + branch
    return stream

def reference(tokens, counts, qkv_weight, qv_bias, out_weight, out_bias, norm_gain, norm_bias, up_weight, up_bias, down_weight, down_bias, cotangent):
    padded_rows = N_CTX * CAP
    position = jnp.arange(padded_rows, dtype=jnp.int32)
    block_of = position // CAP
    slot_of = position - block_of * CAP
    live_mask = (slot_of[None, :] < jnp.take(counts, block_of, axis=1)).astype(jnp.int32)
    live_order = jnp.argsort(1 - live_mask, axis=1, stable=True)[:, :SEQ].astype(jnp.int32)
    image_index = jnp.arange(IMAGES, dtype=jnp.int32)[:, None]
    stream = tokens.astype(jnp.float32)[image_index, live_order]
    grad_in = cotangent.astype(jnp.float32)[image_index, live_order]
    params = tuple((param_value.astype(jnp.float32) for param_value in (qkv_weight, qv_bias, out_weight, out_bias, norm_gain, norm_bias, up_weight, up_bias, down_weight, down_bias)))
    result, pullback = jax.vjp(forward, stream, *params)
    gradients = pullback(grad_in)

    def spread(values):
        return jnp.zeros((IMAGES, padded_rows, D), jnp.float32).at[image_index, live_order].set(values)
    return (spread(result).astype(jnp.bfloat16), spread(gradients[0]), gradients[1], gradients[2], gradients[3], gradients[4], gradients[5], gradients[6], gradients[7], gradients[8], gradients[9], gradients[10])
```

```python
import functools

import jax
import jax.numpy as jnp
from jax import lax
from jax.sharding import PartitionSpec as P

HD = 64
norm_eps = 1e-06
big_negative = -1e30
f32 = jnp.float32
bf16 = jnp.bfloat16


def norm_parts(values):
    centred = values - jnp.mean(values, -1, keepdims=True)
    inverse = lax.rsqrt(jnp.mean(centred * centred, -1, keepdims=True) + norm_eps)
    return centred * inverse, inverse


def norm_backward(grad_out, normal_part, inverse, norm_scale):
    scaled = grad_out * norm_scale
    inner = (
        scaled
        - jnp.mean(scaled, -1, keepdims=True)
        - normal_part * jnp.mean(scaled * normal_part, -1, keepdims=True)
    )
    return (inner * inverse, jnp.sum(grad_out * normal_part, 0), jnp.sum(grad_out, 0))


def gelu_exact(pre_act):
    return jax.nn.gelu(pre_act, approximate=False)


def dot(a, b, contract):
    return lax.dot_general(a, b, ((contract[0:1], contract[1:2]), ((), ())), preferred_element_type=f32)


def split_heads(values):
    return values.reshape(values.shape[0], values.shape[1] // HD, HD)


def attention_forward(query, keys, values, usable):
    rows, width = query.shape
    scores = (
        jnp.einsum("qhd,khd->hqk", split_heads(query), split_heads(keys), preferred_element_type=f32)
        * HD ** (-0.5)
    )
    if usable is not None:
        scores = jnp.where(usable, scores, big_negative)
    top = jnp.max(scores, -1, keepdims=True)
    weights = jnp.exp(scores - top)
    total = jnp.sum(weights, -1, keepdims=True)
    accum = jnp.einsum(
        "hqk,khd->hqd", weights.astype(bf16), split_heads(values), preferred_element_type=f32
    )
    attended = accum / total
    return jnp.transpose(attended, (1, 0, 2)).reshape(rows, width), top + jnp.log(total)


def attention_backward(query, keys, values, grad_attended, attended, log_total, usable):
    rows, width = query.shape
    scale = HD ** (-0.5)
    query_heads, key_heads, value_heads = split_heads(query), split_heads(keys), split_heads(values)
    grad_heads = split_heads(grad_attended)
    delta = jnp.transpose(jnp.sum(grad_heads.astype(f32) * split_heads(attended), -1))[..., None]
    scores = jnp.einsum("qhd,khd->hqk", query_heads, key_heads, preferred_element_type=f32) * scale
    if usable is not None:
        scores = jnp.where(usable, scores, big_negative)
    probs = jnp.exp(scores - log_total)
    grad_probs = jnp.einsum("qhd,khd->hqk", grad_heads, value_heads, preferred_element_type=f32)
    grad_scores = (probs * (grad_probs - delta)).astype(bf16)
    grad_query = (
        jnp.einsum("hqk,khd->qhd", grad_scores, key_heads, preferred_element_type=f32) * scale
    )
    grad_keys = (
        jnp.einsum("hqk,qhd->khd", grad_scores, query_heads, preferred_element_type=f32) * scale
    )
    grad_values = jnp.einsum(
        "hqk,qhd->khd", probs.astype(bf16), grad_heads, preferred_element_type=f32
    )
    length = keys.shape[0]
    return (
        grad_query.reshape(rows, width).astype(bf16),
        grad_keys.reshape(length, width).astype(bf16),
        grad_values.reshape(length, width).astype(bf16),
    )


def local(
    sizes,
    tokens,
    counts,
    qkv_weight,
    qv_bias,
    out_weight,
    out_bias,
    norm_gain,
    norm_bias,
    up_weight,
    up_bias,
    down_weight,
    down_bias,
    cotangent,
):
    n_fsdp, n_ctx, n_tp = sizes
    swap = n_fsdp == n_tp
    head_axis, image_axis = ("fsdp", "tp") if swap else ("tp", "fsdp")
    n_head = n_tp
    pairs = [(f * n_tp + t, t * n_tp + f) for f in range(n_fsdp) for t in range(n_tp)]

    def exchange(value):
        return lax.ppermute(value, ("fsdp", "tp"), pairs) if swap else value

    capacity, width = tokens.shape[1:]
    layers = qkv_weight.shape[0]
    head_width = qkv_weight.shape[3]
    hidden_width = up_weight.shape[2]
    even = n_ctx == 2
    live = counts[0][lax.axis_index("ctx")]
    if even:
        rows = capacity * 4 // 5
        moved = capacity - rows
        kept = rows - moved
        is_full = live > rows
        other_pairs = [(0, 1), (1, 0)]
    else:
        rows = capacity
    share = rows // n_head

    def other(value):
        return lax.ppermute(value, "ctx", other_pairs)

    def packed(layer_no):
        return jnp.concatenate(
            [
                up_weight[layer_no],
                down_weight[layer_no].T,
                out_weight[layer_no].T,
                qkv_weight[layer_no, 0],
                qkv_weight[layer_no, 1],
                qkv_weight[layer_no, 2],
            ],
            1,
        )

    cuts = (0, hidden_width, 2 * hidden_width, 2 * hidden_width + head_width)

    def fetch(layer_no):
        whole = lax.all_gather(
            exchange(packed(layer_no)), (image_axis, "ctx"), axis=0, tiled=True
        )
        return (
            whole[:, cuts[0] : cuts[1]],
            whole[:, cuts[1] : cuts[2]],
            whole[:, cuts[2] : cuts[3]],
            whole[:, cuts[3] :],
        )

    weights = [fetch(layer_no) for layer_no in range(layers)]
    biases = exchange(jnp.concatenate([qv_bias.reshape(-1), up_bias.reshape(-1)]))
    qv_local = biases[: qv_bias.size].reshape(qv_bias.shape)
    up_local = biases[qv_bias.size :].reshape(up_bias.shape)

    both = jnp.stack([tokens[0], cotangent[0]])
    if even:
        arrived = other(both[:, rows:])
        both = jnp.concatenate(
            [both[:, :kept], jnp.where(is_full, both[:, kept:rows], arrived)], 1
        )
        usable = None
    else:
        both = both * (jnp.arange(capacity) < live).astype(bf16)[None, :, None]
        image_counts = exchange(counts[0])
        index = jnp.arange(capacity * n_ctx, dtype=jnp.int32)
        usable = (index % capacity < jnp.repeat(image_counts, capacity))[None, None, :]
    own_live = None
    if not even:
        place = jnp.arange(capacity, dtype=jnp.int32)
        own_live = (place < exchange(counts[0])[lax.axis_index("ctx")]).astype(f32)[:, None]
    start = lax.axis_index("tp") * share
    both = exchange(lax.dynamic_slice_in_dim(both, start, share, 1)).astype(f32)
    stream, grad = both[0], both[1]

    def gather(value):
        return lax.all_gather(value, head_axis, axis=0, tiled=True)

    def scatter(value):
        return lax.psum_scatter(
            value.astype(bf16), head_axis, scatter_dimension=0, tiled=True
        ).astype(f32)

    def finish(value):
        whole = lax.all_gather(exchange(value.astype(bf16)), "tp", axis=0, tiled=True)
        if even:
            tail = whole[kept:]
            arrived = other(tail)
            nothing = jnp.zeros_like(tail)
            return jnp.concatenate(
                [
                    whole[:kept],
                    jnp.where(is_full, tail, nothing),
                    jnp.where(is_full, arrived, nothing),
                ],
                0,
            )[None]
        return (whole * (jnp.arange(capacity) < live).astype(bf16)[:, None])[None]

    saved = []
    for layer_no in range(layers):
        up_full, down_full, out_full, qkv_full = weights[layer_no]
        part_a, inverse_a = norm_parts(stream)
        low_a = gather((part_a * norm_gain[layer_no, 0] + norm_bias[layer_no, 0]).astype(bf16))
        shift = jnp.concatenate(
            [qv_local[layer_no, 0], jnp.zeros((head_width,), f32), qv_local[layer_no, 1]]
        )
        project = (dot(low_a, qkv_full, (1, 0)) + shift).astype(bf16)
        query, own_kv = project[:, :head_width], project[:, head_width:]
        if even:
            all_kv = jnp.concatenate([own_kv, other(own_kv)], 0)
        else:
            all_kv = lax.all_gather(own_kv, "ctx", axis=0, tiled=True)
        keys, values = all_kv[:, :head_width], all_kv[:, head_width:]
        attended, log_total = attention_forward(query, keys, values, usable)
        low_attended = attended.astype(bf16)
        hidden = stream + scatter(dot(low_attended, out_full, (1, 1))) + out_bias[layer_no]
        part_c, inverse_c = norm_parts(hidden)
        low_c = gather((part_c * norm_gain[layer_no, 1] + norm_bias[layer_no, 1]).astype(bf16))
        pre_act = dot(low_c, up_full, (1, 0)) + up_local[layer_no]
        low_z = gelu_exact(pre_act).astype(bf16)
        stream = hidden + scatter(dot(low_z, down_full, (1, 1))) + down_bias[layer_no]
        saved.append(
            (part_a, inverse_a, low_a, query, keys, values, attended, log_total, low_attended)
            + (part_c, inverse_c, low_c, pre_act, low_z)
        )
    block_output = finish(stream)

    def owned(value):
        return exchange(
            lax.psum_scatter(
                value.astype(bf16), (image_axis, "ctx"), scatter_dimension=0, tiled=True
            )
        ).astype(f32)

    outs = [None] * layers
    head_place = lax.axis_index(head_axis)
    for layer_no in reversed(range(layers)):
        up_full, down_full, out_full, qkv_full = weights[layer_no]
        (part_a, inverse_a, low_a, query, keys, values, attended, log_total, low_attended) = saved[
            layer_no
        ][:9]
        part_c, inverse_c, low_c, pre_act, low_z = saved[layer_no][9:]
        share_m = grad.astype(bf16)
        low_m = gather(share_m)
        grad_z = dot(low_m, down_full, (1, 0))
        _, gelu_pull = jax.vjp(gelu_exact, pre_act)
        low_dpre = gelu_pull(grad_z)[0].astype(bf16)
        if own_live is not None:
            low_dpre = low_dpre * own_live.astype(bf16)
        grad_c = scatter(dot(low_dpre, up_full, (1, 1)))
        mlp_grads = jnp.concatenate(
            [dot(low_c, low_dpre, (0, 0)), dot(low_m, low_z, (0, 0))], 1
        ).astype(bf16)
        mlp_owned = owned(mlp_grads)
        grad_from_c, gain_two, shift_two = norm_backward(
            grad_c, part_c, inverse_c, norm_gain[layer_no, 1]
        )
        grad_h = grad + grad_from_c
        share_mix = grad_h.astype(bf16)
        low_mix = gather(share_mix)
        grad_attended = dot(low_mix, out_full, (1, 0)).astype(bf16)
        grad_query, grad_keys, grad_values = attention_backward(
            query, keys, values, grad_attended, attended, log_total, usable
        )
        grad_kv = jnp.concatenate([grad_keys, grad_values], 1)
        if even:
            grad_kv = (grad_kv[:rows].astype(f32) + other(grad_kv[rows:]).astype(f32)).astype(bf16)
        else:
            grad_kv = lax.psum_scatter(grad_kv, "ctx", scatter_dimension=0, tiled=True)
        stacked = jnp.concatenate([grad_query, grad_kv], 1)
        grad_a = scatter(dot(stacked, qkv_full, (1, 1)))
        att_grads = jnp.concatenate(
            [dot(low_mix, low_attended, (0, 0)), dot(low_a, stacked, (0, 0))], 1
        ).astype(bf16)
        att_owned = owned(att_grads)
        grad_from_a, gain_one, shift_one = norm_backward(
            grad_a, part_a, inverse_a, norm_gain[layer_no, 0]
        )
        grad = grad_h + grad_from_a
        qkv_sums = jnp.sum(stacked.astype(f32), 0)
        placed = jnp.concatenate(
            [
                qkv_sums[:head_width],
                qkv_sums[2 * head_width :],
                jnp.sum(low_dpre.astype(f32), 0),
            ]
        )
        slots = jnp.where(jnp.arange(n_head)[:, None] == head_place, placed[None], 0.0)
        summed = lax.psum(
            jnp.concatenate(
                [
                    gain_one,
                    gain_two,
                    shift_one,
                    shift_two,
                    jnp.sum(share_mix.astype(f32), 0),
                    jnp.sum(share_m.astype(f32), 0),
                    slots.reshape(-1),
                ]
            ),
            ("fsdp", "ctx", "tp"),
        )
        shared = summed[: 6 * width].reshape(6, width)
        mine = lax.dynamic_index_in_dim(
            summed[6 * width :].reshape(n_head, -1), lax.axis_index("tp"), 0, keepdims=False
        )
        outs[layer_no] = (
            jnp.transpose(
                att_owned[:, head_width:].reshape(att_owned.shape[0], 3, head_width), (1, 0, 2)
            ),
            mine[: 2 * head_width].reshape(2, head_width),
            att_owned[:, :head_width].T,
            shared[4],
            shared[0:2],
            shared[2:4],
            mlp_owned[:, :hidden_width],
            mine[2 * head_width :],
            mlp_owned[:, hidden_width:].T,
            shared[5],
        )
    grad_tokens = finish(grad).astype(f32)
    return (block_output, grad_tokens) + tuple(jnp.stack(entry) for entry in zip(*outs))


def solution(mesh):
    sizes = tuple(mesh.shape[name] for name in ("fsdp", "ctx", "tp"))
    return jax.shard_map(
        functools.partial(local, sizes),
        mesh=mesh,
        in_specs=(
            P("fsdp", "ctx", None),
            P("fsdp", None),
            P(None, None, ("fsdp", "ctx"), "tp"),
            P(None, None, "tp"),
            P(None, "tp", ("fsdp", "ctx")),
            P(),
            P(),
            P(),
            P(None, ("fsdp", "ctx"), "tp"),
            P(None, "tp"),
            P(None, "tp", ("fsdp", "ctx")),
            P(),
            P("fsdp", "ctx", None),
        ),
        out_specs=(
            P("fsdp", "ctx", None),
            P("fsdp", "ctx", None),
            P(None, None, ("fsdp", "ctx"), "tp"),
            P(None, None, "tp"),
            P(None, "tp", ("fsdp", "ctx")),
            P(),
            P(),
            P(),
            P(None, ("fsdp", "ctx"), "tp"),
            P(None, "tp"),
            P(None, "tp", ("fsdp", "ctx")),
            P(),
        ),
        check_vma=False,
    )
```

```python
import functools

import jax
import jax.numpy as jnp
from jax import lax
from jax.experimental import pallas as pl
from jax.experimental.pallas import tpu as pltpu
from jax.sharding import PartitionSpec as P

HD = 64
norm_eps = 1e-06
big_negative = -1e30
f32 = jnp.float32
bf16 = jnp.bfloat16


def norm_parts(values):
    centred = values - jnp.mean(values, -1, keepdims=True)
    inverse = lax.rsqrt(jnp.mean(centred * centred, -1, keepdims=True) + norm_eps)
    return centred * inverse, inverse


def norm_backward(grad_out, normal_part, inverse, norm_scale):
    scaled = grad_out * norm_scale
    inner = (
        scaled
        - jnp.mean(scaled, -1, keepdims=True)
        - normal_part * jnp.mean(scaled * normal_part, -1, keepdims=True)
    )
    return (inner * inverse, jnp.sum(grad_out * normal_part, 0), jnp.sum(grad_out, 0))


def gelu_exact(pre_act):
    return jax.nn.gelu(pre_act, approximate=False)


def dot(a, b, contract):
    return lax.dot_general(a, b, ((contract[0:1], contract[1:2]), ((), ())), preferred_element_type=f32)


def split_heads(values):
    return values.reshape(values.shape[0], values.shape[1] // HD, HD)


def attention_forward(query, keys, values, usable):
    rows, width = query.shape
    scores = (
        jnp.einsum("qhd,khd->hqk", split_heads(query), split_heads(keys), preferred_element_type=f32)
        * HD ** (-0.5)
    )
    if usable is not None:
        scores = jnp.where(usable, scores, big_negative)
    top = jnp.max(scores, -1, keepdims=True)
    weights = jnp.exp(scores - top)
    total = jnp.sum(weights, -1, keepdims=True)
    accum = jnp.einsum(
        "hqk,khd->hqd", weights.astype(bf16), split_heads(values), preferred_element_type=f32
    )
    attended = accum / total
    return jnp.transpose(attended, (1, 0, 2)).reshape(rows, width), top + jnp.log(total)


def attention_backward(query, keys, values, grad_attended, attended, log_total, usable):
    rows, width = query.shape
    scale = HD ** (-0.5)
    query_heads, key_heads, value_heads = split_heads(query), split_heads(keys), split_heads(values)
    grad_heads = split_heads(grad_attended)
    delta = jnp.transpose(jnp.sum(grad_heads.astype(f32) * split_heads(attended), -1))[..., None]
    scores = jnp.einsum("qhd,khd->hqk", query_heads, key_heads, preferred_element_type=f32) * scale
    if usable is not None:
        scores = jnp.where(usable, scores, big_negative)
    probs = jnp.exp(scores - log_total)
    grad_probs = jnp.einsum("qhd,khd->hqk", grad_heads, value_heads, preferred_element_type=f32)
    grad_scores = (probs * (grad_probs - delta)).astype(bf16)
    grad_query = (
        jnp.einsum("hqk,khd->qhd", grad_scores, key_heads, preferred_element_type=f32) * scale
    )
    grad_keys = (
        jnp.einsum("hqk,qhd->khd", grad_scores, query_heads, preferred_element_type=f32) * scale
    )
    grad_values = jnp.einsum(
        "hqk,qhd->khd", probs.astype(bf16), grad_heads, preferred_element_type=f32
    )
    length = keys.shape[0]
    return (
        grad_query.reshape(rows, width).astype(bf16),
        grad_keys.reshape(length, width).astype(bf16),
        grad_values.reshape(length, width).astype(bf16),
    )


MESH = pl.DeviceIdType.MESH


def meet(partners):
    barrier = pltpu.get_barrier_semaphore()
    for partner in partners:
        pl.semaphore_signal(barrier, inc=1, device_id=partner, device_id_type=MESH)
    pl.semaphore_wait(barrier, len(partners))


def send(source, target, partner, sems, place):
    copy = pltpu.make_async_remote_copy(
        src_ref=source,
        dst_ref=target,
        send_sem=sems.at[0, place],
        recv_sem=sems.at[1, place],
        device_id=partner,
        device_id_type=MESH,
    )
    copy.start()
    return copy


def group_kernel(axis, middle, with_gather, n_in, n_out, partial, *refs):
    ins, outs = refs[:n_in], refs[n_in : n_in + n_out]
    scratch = refs[n_in + n_out :]
    near_recv, far_send, far_recv, near_sems, far_sem = scratch[:5]
    me = lax.axis_index(axis)
    near_at, far_at = me + 1 - 2 * (me % 2), (me + 2) % 4
    cross_at = (near_at + 2) % 4
    near, far = {axis: near_at}, {axis: far_at}
    share = near_recv.shape[1]
    meet((near, far))

    def rows_of(place):
        return pl.ds(pl.multiple_of(place * share, share), share)

    first = send(partial.at[rows_of(cross_at)], near_recv.at[0], near, near_sems, 0)
    second = send(partial.at[rows_of(near_at)], near_recv.at[1], near, near_sems, 1)
    first.wait()
    far_send[...] = (
        partial[rows_of(far_at), :].astype(f32) + near_recv[0].astype(f32)
    ).astype(bf16)
    across = send(far_send, far_recv, far, far_sem, 0)
    second.wait()
    across.wait()
    total = (
        partial[rows_of(me), :].astype(f32)
        + near_recv[1].astype(f32)
        + far_recv[...].astype(f32)
    )
    low = middle(total, ins, outs)
    if not with_gather:
        return
    whole, gather_sems = scratch[5:]
    whole[me] = low
    over = send(whole.at[me], whole.at[me], far, gather_sems, 0)
    beside = send(whole.at[me], whole.at[me], near, gather_sems, 1)
    over.wait()
    onward = send(whole.at[far_at], whole.at[far_at], near, gather_sems, 2)
    beside.wait()
    onward.wait()
    for place in range(4):
        outs[-1][place * share : (place + 1) * share, :] = whole[place]


def group_call(name, number, axis, middle, with_gather, partial, ins, outs):
    rows, width = partial.shape
    share = rows // 4
    shapes = [jax.ShapeDtypeStruct(shape, f32) for shape in outs]
    if with_gather:
        shapes.append(jax.ShapeDtypeStruct((rows, width), bf16))
    scratch = [
        pltpu.VMEM((2, share, width), bf16),
        pltpu.VMEM((share, width), bf16),
        pltpu.VMEM((share, width), bf16),
        pltpu.SemaphoreType.DMA((2, 2)),
        pltpu.SemaphoreType.DMA((2, 1)),
    ]
    if with_gather:
        scratch += [pltpu.VMEM((4, share, width), bf16), pltpu.SemaphoreType.DMA((2, 3))]
    vmem = pl.BlockSpec(memory_space=pltpu.VMEM)
    return pl.pallas_call(
        functools.partial(group_kernel, axis, middle, with_gather, len(ins), len(shapes)),
        out_shape=shapes,
        in_specs=[vmem] * (1 + len(ins)),
        out_specs=[vmem] * len(shapes),
        scratch_shapes=scratch,
        compiler_params=pltpu.CompilerParams(
            collective_id=number, has_side_effects=True, vmem_limit_bytes=32 * 1024 * 1024
        ),
        cost_estimate=pl.CostEstimate(
            flops=rows * width * 10, bytes_accessed=rows * width * 8, transcendentals=0
        ),
        name=name,
    )(partial, *ins)


def forward_middle(total, ins, outs):
    stream, consts = ins
    hidden = stream[...] + total + consts[0:1, :]
    normal_part, inverse = norm_parts(hidden)
    outs[0][...] = hidden
    outs[1][...] = normal_part
    outs[2][...] = inverse
    return (normal_part * consts[1:2, :] + consts[2:3, :]).astype(bf16)


def last_middle(total, ins, outs):
    stream, consts, low = ins
    outs[0][...] = stream[...] + total + consts[0:1, :]
    return low[...]


def backward_middle(total, ins, outs):
    grad, normal_part, inverse, consts = ins
    part = normal_part[...]
    scaled = total * consts[1:2, :]
    inner = (
        scaled
        - jnp.mean(scaled, -1, keepdims=True)
        - part * jnp.mean(scaled * part, -1, keepdims=True)
    )
    updated = grad[...] + inner * inverse[...]
    low = updated.astype(bf16)
    outs[0][...] = updated
    outs[1][0:1, :] = jnp.sum(total * part, 0, keepdims=True)
    outs[1][1:2, :] = jnp.sum(total, 0, keepdims=True)
    outs[1][2:3, :] = jnp.sum(low.astype(f32), 0, keepdims=True)
    outs[1][3:8, :] = jnp.zeros((5, total.shape[1]), f32)
    return low


def everyone_kernel(steps, value, out, sending, arriving, sems):
    partners = []
    for axis, stride in steps:
        at = lax.axis_index(axis)
        partners.append({axis: at + stride - 2 * stride * ((at // stride) % 2)})
    meet(partners)
    out[...] = value[...]
    for place, partner in enumerate(partners):
        sending[place] = out[...]
        send(sending.at[place], arriving.at[place], partner, sems, place).wait()
        out[...] = out[...] + arriving[place]


def everyone_call(number, sizes, value):
    steps = []
    for axis, size in zip(("fsdp", "ctx", "tp"), sizes):
        stride = 1
        while stride < size:
            steps.append((axis, stride))
            stride *= 2
    vmem = pl.BlockSpec(memory_space=pltpu.VMEM)
    held = pltpu.VMEM((len(steps),) + value.shape, f32)
    return pl.pallas_call(
        functools.partial(everyone_kernel, steps),
        out_shape=jax.ShapeDtypeStruct(value.shape, f32),
        in_specs=[vmem],
        out_specs=vmem,
        scratch_shapes=[held, held, pltpu.SemaphoreType.DMA((2, len(steps)))],
        compiler_params=pltpu.CompilerParams(
            collective_id=number, has_side_effects=True, vmem_limit_bytes=32 * 1024 * 1024
        ),
        name="sum_everywhere",
    )(value)


def local(
    sizes,
    tokens,
    counts,
    qkv_weight,
    qv_bias,
    out_weight,
    out_bias,
    norm_gain,
    norm_bias,
    up_weight,
    up_bias,
    down_weight,
    down_bias,
    cotangent,
):
    n_fsdp, n_ctx, n_tp = sizes
    swap = n_fsdp == n_tp
    head_axis, image_axis = ("fsdp", "tp") if swap else ("tp", "fsdp")
    n_head = n_tp
    pairs = [(f * n_tp + t, t * n_tp + f) for f in range(n_fsdp) for t in range(n_tp)]

    def exchange(value):
        return lax.ppermute(value, ("fsdp", "tp"), pairs) if swap else value

    capacity, width = tokens.shape[1:]
    layers = qkv_weight.shape[0]
    head_width = qkv_weight.shape[3]
    hidden_width = up_weight.shape[2]
    even = n_ctx == 2
    live = counts[0][lax.axis_index("ctx")]
    if even:
        rows = capacity * 4 // 5
        moved = capacity - rows
        kept = rows - moved
        is_full = live > rows
        other_pairs = [(0, 1), (1, 0)]
    else:
        rows = capacity
    share = rows // n_head

    def other(value):
        return lax.ppermute(value, "ctx", other_pairs)

    def packed(layer_no):
        return jnp.concatenate(
            [
                up_weight[layer_no],
                down_weight[layer_no].T,
                out_weight[layer_no].T,
                qkv_weight[layer_no, 0],
                qkv_weight[layer_no, 1],
                qkv_weight[layer_no, 2],
            ],
            1,
        )

    cuts = (0, hidden_width, 2 * hidden_width, 2 * hidden_width + head_width)

    def fetch(layer_no):
        mine = packed(layer_no)

        def spread(piece):
            return lax.all_gather(exchange(piece), (image_axis, "ctx"), axis=0, tiled=True)

        att, mlp = spread(mine[:, cuts[2] :]), spread(mine[:, : cuts[2]])
        return (
            mlp[:, :hidden_width],
            mlp[:, hidden_width:],
            att[:, :head_width],
            att[:, head_width:],
        )

    weights = [fetch(layer_no) for layer_no in range(layers)]
    biases = exchange(jnp.concatenate([qv_bias.reshape(-1), up_bias.reshape(-1)]))
    qv_local = biases[: qv_bias.size].reshape(qv_bias.shape)
    up_local = biases[qv_bias.size :].reshape(up_bias.shape)

    both = jnp.stack([tokens[0], cotangent[0]])
    if even:
        arrived = other(both[:, rows:])
        both = jnp.concatenate(
            [both[:, :kept], jnp.where(is_full, both[:, kept:rows], arrived)], 1
        )
        usable = None
    else:
        both = both * (jnp.arange(capacity) < live).astype(bf16)[None, :, None]
        image_counts = exchange(counts[0])
        index = jnp.arange(capacity * n_ctx, dtype=jnp.int32)
        usable = (index % capacity < jnp.repeat(image_counts, capacity))[None, None, :]
    own_live = None
    if not even:
        place = jnp.arange(capacity, dtype=jnp.int32)
        own_live = (place < exchange(counts[0])[lax.axis_index("ctx")]).astype(f32)[:, None]
    start = lax.axis_index("tp") * share
    both = exchange(lax.dynamic_slice_in_dim(both, start, share, 1)).astype(f32)
    stream, grad = both[0], both[1]

    def gather(value):
        return lax.all_gather(value, head_axis, axis=0, tiled=True)

    def scatter(value):
        return lax.psum_scatter(
            value.astype(bf16), head_axis, scatter_dimension=0, tiled=True
        ).astype(f32)

    use_kernels = swap and even and n_head == 4 and share % 16 == 0

    def constants(*entries):
        return jnp.pad(jnp.stack(entries), ((0, 8 - len(entries)), (0, 0)))

    wide, thin = (share, width), (share, 1)

    def forward_join(partial, base, bias, gain, shift):
        if use_kernels:
            return group_call(
                "sum_norm_gather", 0, head_axis, forward_middle, True, partial.astype(bf16),
                (base, constants(bias, gain, shift)), (wide, wide, thin),
            )
        total = base + scatter(partial) + bias
        normal_part, inverse = norm_parts(total)
        return total, normal_part, inverse, gather((normal_part * gain + shift).astype(bf16))

    def last_join(partial, base, bias, low):
        if use_kernels:
            return group_call(
                "sum_then_gather", 1, head_axis, last_middle, True, partial.astype(bf16),
                (base, constants(bias), low), (wide,),
            )
        return base + scatter(partial) + bias, gather(low)

    def backward_join(partial, base, normal_part, inverse, gain, last):
        if use_kernels:
            updated, sums, *low = group_call(
                "sum_norm_last" if last else "sum_norm_back", 3 if last else 2, head_axis,
                backward_middle, not last, partial.astype(bf16),
                (base, normal_part, inverse, constants(gain, gain)), (wide, (8, width)),
            )
            return updated, sums[0], sums[1], sums[2], (low[0] if low else None)
        change, gain_sum, shift_sum = norm_backward(scatter(partial), normal_part, inverse, gain)
        updated = base + change
        low = updated.astype(bf16)
        low_sum = jnp.sum(low.astype(f32), 0)
        return updated, gain_sum, shift_sum, low_sum, (None if last else gather(low))

    def everyone(value):
        if use_kernels:
            return everyone_call(4, sizes, value.reshape(-1, 128)).reshape(value.shape)
        return lax.psum(value, ("fsdp", "ctx", "tp"))

    def finish(value):
        whole = lax.all_gather(exchange(value.astype(bf16)), "tp", axis=0, tiled=True)
        if even:
            tail = whole[kept:]
            arrived = other(tail)
            nothing = jnp.zeros_like(tail)
            return jnp.concatenate(
                [
                    whole[:kept],
                    jnp.where(is_full, tail, nothing),
                    jnp.where(is_full, arrived, nothing),
                ],
                0,
            )[None]
        return (whole * (jnp.arange(capacity) < live).astype(bf16)[:, None])[None]

    saved = []
    part_a, inverse_a = norm_parts(stream)
    low_a = gather((part_a * norm_gain[0, 0] + norm_bias[0, 0]).astype(bf16))
    share_m = grad.astype(bf16)
    for layer_no in range(layers):
        up_full, down_full, out_full, qkv_full = weights[layer_no]
        shift = jnp.concatenate(
            [qv_local[layer_no, 0], jnp.zeros((head_width,), f32), qv_local[layer_no, 1]]
        )
        project = (dot(low_a, qkv_full, (1, 0)) + shift).astype(bf16)
        query, own_kv = project[:, :head_width], project[:, head_width:]
        if even:
            all_kv = jnp.concatenate([own_kv, other(own_kv)], 0)
        else:
            all_kv = lax.all_gather(own_kv, "ctx", axis=0, tiled=True)
        keys, values = all_kv[:, :head_width], all_kv[:, head_width:]
        attended, log_total = attention_forward(query, keys, values, usable)
        low_attended = attended.astype(bf16)
        hidden, part_c, inverse_c, low_c = forward_join(
            dot(low_attended, out_full, (1, 1)),
            stream,
            out_bias[layer_no],
            norm_gain[layer_no, 1],
            norm_bias[layer_no, 1],
        )
        pre_act = dot(low_c, up_full, (1, 0)) + up_local[layer_no]
        low_z = gelu_exact(pre_act).astype(bf16)
        saved.append(
            (part_a, inverse_a, low_a, query, keys, values, attended, log_total, low_attended)
            + (part_c, inverse_c, low_c, pre_act, low_z)
        )
        branch = dot(low_z, down_full, (1, 1))
        if layer_no + 1 < layers:
            stream, part_a, inverse_a, low_a = forward_join(
                branch,
                hidden,
                down_bias[layer_no],
                norm_gain[layer_no + 1, 0],
                norm_bias[layer_no + 1, 0],
            )
        else:
            stream, low_m = last_join(branch, hidden, down_bias[layer_no], share_m)
    block_output = finish(stream)

    def owned(value):
        return exchange(
            lax.psum_scatter(
                value.astype(bf16), (image_axis, "ctx"), scatter_dimension=0, tiled=True
            )
        ).astype(f32)

    outs = [None] * layers
    smalls = [None] * layers
    sum_m = jnp.sum(share_m.astype(f32), 0)
    head_place = lax.axis_index(head_axis)
    for layer_no in reversed(range(layers)):
        up_full, down_full, out_full, qkv_full = weights[layer_no]
        (part_a, inverse_a, low_a, query, keys, values, attended, log_total, low_attended) = saved[
            layer_no
        ][:9]
        part_c, inverse_c, low_c, pre_act, low_z = saved[layer_no][9:]
        grad_z = dot(low_m, down_full, (1, 0))
        _, gelu_pull = jax.vjp(gelu_exact, pre_act)
        low_dpre = gelu_pull(grad_z)[0].astype(bf16)
        if own_live is not None:
            low_dpre = low_dpre * own_live.astype(bf16)
        partial_c = dot(low_dpre, up_full, (1, 1)).astype(bf16)
        mlp_grads = jnp.concatenate(
            [dot(low_c, low_dpre, (0, 0)), dot(low_m, low_z, (0, 0))], 1
        ).astype(bf16)
        partial_c, mlp_grads = lax.optimization_barrier((partial_c, mlp_grads))
        mlp_owned = owned(mlp_grads)
        grad_h, gain_two, shift_two, sum_mix, low_mix = backward_join(
            partial_c, grad, part_c, inverse_c, norm_gain[layer_no, 1], False
        )
        grad_attended = dot(low_mix, out_full, (1, 0)).astype(bf16)
        grad_query, grad_keys, grad_values = attention_backward(
            query, keys, values, grad_attended, attended, log_total, usable
        )
        grad_kv = jnp.concatenate([grad_keys, grad_values], 1)
        if even:
            grad_kv = (grad_kv[:rows].astype(f32) + other(grad_kv[rows:]).astype(f32)).astype(bf16)
        else:
            grad_kv = lax.psum_scatter(grad_kv, "ctx", scatter_dimension=0, tiled=True)
        stacked = jnp.concatenate([grad_query, grad_kv], 1)
        partial_a = dot(stacked, qkv_full, (1, 1)).astype(bf16)
        att_grads = jnp.concatenate(
            [dot(low_mix, low_attended, (0, 0)), dot(low_a, stacked, (0, 0))], 1
        ).astype(bf16)
        partial_a, att_grads = lax.optimization_barrier((partial_a, att_grads))
        att_owned = owned(att_grads)
        sum_m_here = sum_m
        grad, gain_one, shift_one, sum_m, low_m = backward_join(
            partial_a, grad_h, part_a, inverse_a, norm_gain[layer_no, 0], layer_no == 0
        )
        qkv_sums = jnp.sum(stacked.astype(f32), 0)
        placed = jnp.concatenate(
            [
                qkv_sums[:head_width],
                qkv_sums[2 * head_width :],
                jnp.sum(low_dpre.astype(f32), 0),
            ]
        )
        slots = jnp.where(jnp.arange(n_head)[:, None] == head_place, placed[None], 0.0)
        smalls[layer_no] = jnp.concatenate(
            [gain_one, gain_two, shift_one, shift_two, sum_mix, sum_m_here, slots.reshape(-1)]
        )
        outs[layer_no] = (
            jnp.transpose(
                att_owned[:, head_width:].reshape(att_owned.shape[0], 3, head_width), (1, 0, 2)
            ),
            att_owned[:, :head_width].T,
            mlp_owned[:, :hidden_width],
            mlp_owned[:, hidden_width:].T,
        )
    grad_tokens = finish(grad).astype(f32)
    summed = everyone(jnp.stack(smalls))
    shared = summed[:, : 6 * width].reshape(layers, 6, width)
    mine = lax.dynamic_index_in_dim(
        summed[:, 6 * width :].reshape(layers, n_head, -1), lax.axis_index("tp"), 1, keepdims=False
    )
    grad_qkv, grad_out, grad_up, grad_down = (jnp.stack(entry) for entry in zip(*outs))
    return (
        block_output,
        grad_tokens,
        grad_qkv,
        mine[:, : 2 * head_width].reshape(layers, 2, head_width),
        grad_out,
        shared[:, 4],
        shared[:, 0:2],
        shared[:, 2:4],
        grad_up,
        mine[:, 2 * head_width :],
        grad_down,
        shared[:, 5],
    )


def solution(mesh):
    sizes = tuple(mesh.shape[name] for name in ("fsdp", "ctx", "tp"))
    return jax.shard_map(
        functools.partial(local, sizes),
        mesh=mesh,
        in_specs=(
            P("fsdp", "ctx", None),
            P("fsdp", None),
            P(None, None, ("fsdp", "ctx"), "tp"),
            P(None, None, "tp"),
            P(None, "tp", ("fsdp", "ctx")),
            P(),
            P(),
            P(),
            P(None, ("fsdp", "ctx"), "tp"),
            P(None, "tp"),
            P(None, "tp", ("fsdp", "ctx")),
            P(),
            P("fsdp", "ctx", None),
        ),
        out_specs=(
            P("fsdp", "ctx", None),
            P("fsdp", "ctx", None),
            P(None, None, ("fsdp", "ctx"), "tp"),
            P(None, None, "tp"),
            P(None, "tp", ("fsdp", "ctx")),
            P(),
            P(),
            P(),
            P(None, ("fsdp", "ctx"), "tp"),
            P(None, "tp"),
            P(None, "tp", ("fsdp", "ctx")),
            P(),
        ),
        check_vma=False,
    )
```

```python
import functools

import jax
import jax.numpy as jnp
from jax import lax
from jax.experimental import pallas as pl
from jax.experimental.pallas import tpu as pltpu
from jax.sharding import PartitionSpec as P

HD = 64
norm_eps = 1e-06
big_negative = -1e30
f32 = jnp.float32
bf16 = jnp.bfloat16


def norm_parts(values):
    centred = values - jnp.mean(values, -1, keepdims=True)
    inverse = lax.rsqrt(jnp.mean(centred * centred, -1, keepdims=True) + norm_eps)
    return centred * inverse, inverse


def norm_backward(grad_out, normal_part, inverse, norm_scale):
    scaled = grad_out * norm_scale
    inner = (
        scaled
        - jnp.mean(scaled, -1, keepdims=True)
        - normal_part * jnp.mean(scaled * normal_part, -1, keepdims=True)
    )
    return (inner * inverse, jnp.sum(grad_out * normal_part, 0), jnp.sum(grad_out, 0))


def gelu_exact(pre_act):
    return jax.nn.gelu(pre_act, approximate=False)


def dot(a, b, contract):
    return lax.dot_general(a, b, ((contract[0:1], contract[1:2]), ((), ())), preferred_element_type=f32)


def split_heads(values):
    return values.reshape(values.shape[0], values.shape[1] // HD, HD)


def attention_forward(query, keys, values, usable):
    rows, width = query.shape
    scores = (
        jnp.einsum("qhd,khd->hqk", split_heads(query), split_heads(keys), preferred_element_type=f32)
        * HD ** (-0.5)
    )
    if usable is not None:
        scores = jnp.where(usable, scores, big_negative)
    top = jnp.max(scores, -1, keepdims=True)
    weights = jnp.exp(scores - top)
    total = jnp.sum(weights, -1, keepdims=True)
    accum = jnp.einsum(
        "hqk,khd->hqd", weights.astype(bf16), split_heads(values), preferred_element_type=f32
    )
    attended = accum / total
    return jnp.transpose(attended, (1, 0, 2)).reshape(rows, width), top + jnp.log(total)


def attention_backward(query, keys, values, grad_attended, attended, log_total, usable):
    rows, width = query.shape
    scale = HD ** (-0.5)
    query_heads, key_heads, value_heads = split_heads(query), split_heads(keys), split_heads(values)
    grad_heads = split_heads(grad_attended)
    delta = jnp.transpose(jnp.sum(grad_heads.astype(f32) * split_heads(attended), -1))[..., None]
    scores = jnp.einsum("qhd,khd->hqk", query_heads, key_heads, preferred_element_type=f32) * scale
    if usable is not None:
        scores = jnp.where(usable, scores, big_negative)
    probs = jnp.exp(scores - log_total)
    grad_probs = jnp.einsum("qhd,khd->hqk", grad_heads, value_heads, preferred_element_type=f32)
    grad_scores = (probs * (grad_probs - delta)).astype(bf16)
    grad_query = (
        jnp.einsum("hqk,khd->qhd", grad_scores, key_heads, preferred_element_type=f32) * scale
    )
    grad_keys = (
        jnp.einsum("hqk,qhd->khd", grad_scores, query_heads, preferred_element_type=f32) * scale
    )
    grad_values = jnp.einsum(
        "hqk,qhd->khd", probs.astype(bf16), grad_heads, preferred_element_type=f32
    )
    length = keys.shape[0]
    return (
        grad_query.reshape(rows, width).astype(bf16),
        grad_keys.reshape(length, width).astype(bf16),
        grad_values.reshape(length, width).astype(bf16),
    )


MESH = pl.DeviceIdType.MESH


def meet(partners):
    barrier = pltpu.get_barrier_semaphore()
    for partner in partners:
        pl.semaphore_signal(barrier, inc=1, device_id=partner, device_id_type=MESH)
    pl.semaphore_wait(barrier, len(partners))


def send(source, target, partner, sems, place):
    copy = pltpu.make_async_remote_copy(
        src_ref=source,
        dst_ref=target,
        send_sem=sems.at[0, place],
        recv_sem=sems.at[1, place],
        device_id=partner,
        device_id_type=MESH,
    )
    copy.start()
    return copy


def group_kernel(axis, middle, with_gather, n_in, n_out, partial, *refs):
    ins, outs = refs[:n_in], refs[n_in : n_in + n_out]
    scratch = refs[n_in + n_out :]
    near_recv, far_send, far_recv, near_sems, far_sem = scratch[:5]
    me = lax.axis_index(axis)
    near_at, far_at = me + 1 - 2 * (me % 2), (me + 2) % 4
    cross_at = (near_at + 2) % 4
    near, far = {axis: near_at}, {axis: far_at}
    share = near_recv.shape[1]
    meet((near, far))

    def rows_of(place):
        return pl.ds(pl.multiple_of(place * share, share), share)

    first = send(partial.at[rows_of(cross_at)], near_recv.at[0], near, near_sems, 0)
    second = send(partial.at[rows_of(near_at)], near_recv.at[1], near, near_sems, 1)
    first.wait()
    far_send[...] = (
        partial[rows_of(far_at), :].astype(f32) + near_recv[0].astype(f32)
    ).astype(bf16)
    across = send(far_send, far_recv, far, far_sem, 0)
    second.wait()
    across.wait()
    total = (
        partial[rows_of(me), :].astype(f32)
        + near_recv[1].astype(f32)
        + far_recv[...].astype(f32)
    )
    low = middle(total, ins, outs)
    if not with_gather:
        return
    whole, gather_sems = scratch[5:]
    whole[me] = low
    over = send(whole.at[me], whole.at[me], far, gather_sems, 0)
    beside = send(whole.at[me], whole.at[me], near, gather_sems, 1)
    over.wait()
    onward = send(whole.at[far_at], whole.at[far_at], near, gather_sems, 2)
    beside.wait()
    onward.wait()
    for place in range(4):
        outs[-1][place * share : (place + 1) * share, :] = whole[place]


def group_call(name, number, axis, middle, with_gather, partial, ins, outs):
    rows, width = partial.shape
    share = rows // 4
    shapes = [jax.ShapeDtypeStruct(shape, f32) for shape in outs]
    if with_gather:
        shapes.append(jax.ShapeDtypeStruct((rows, width), bf16))
    scratch = [
        pltpu.VMEM((2, share, width), bf16),
        pltpu.VMEM((share, width), bf16),
        pltpu.VMEM((share, width), bf16),
        pltpu.SemaphoreType.DMA((2, 2)),
        pltpu.SemaphoreType.DMA((2, 1)),
    ]
    if with_gather:
        scratch += [pltpu.VMEM((4, share, width), bf16), pltpu.SemaphoreType.DMA((2, 3))]
    vmem = pl.BlockSpec(memory_space=pltpu.VMEM)
    return pl.pallas_call(
        functools.partial(group_kernel, axis, middle, with_gather, len(ins), len(shapes)),
        out_shape=shapes,
        in_specs=[vmem] * (1 + len(ins)),
        out_specs=[vmem] * len(shapes),
        scratch_shapes=scratch,
        compiler_params=pltpu.CompilerParams(
            collective_id=number, has_side_effects=True, vmem_limit_bytes=32 * 1024 * 1024
        ),
        cost_estimate=pl.CostEstimate(
            flops=rows * width * 10, bytes_accessed=rows * width * 8, transcendentals=0
        ),
        name=name,
    )(partial, *ins)


def forward_middle(total, ins, outs):
    stream, consts = ins
    hidden = stream[...] + total + consts[0:1, :]
    normal_part, inverse = norm_parts(hidden)
    outs[0][...] = hidden
    outs[1][...] = normal_part
    outs[2][...] = inverse
    return (normal_part * consts[1:2, :] + consts[2:3, :]).astype(bf16)


def last_middle(total, ins, outs):
    stream, consts, low = ins
    outs[0][...] = stream[...] + total + consts[0:1, :]
    return low[...]


def backward_middle(total, ins, outs):
    grad, normal_part, inverse, consts = ins
    part = normal_part[...]
    scaled = total * consts[1:2, :]
    inner = (
        scaled
        - jnp.mean(scaled, -1, keepdims=True)
        - part * jnp.mean(scaled * part, -1, keepdims=True)
    )
    updated = grad[...] + inner * inverse[...]
    low = updated.astype(bf16)
    outs[0][...] = updated
    outs[1][0:1, :] = jnp.sum(total * part, 0, keepdims=True)
    outs[1][1:2, :] = jnp.sum(total, 0, keepdims=True)
    outs[1][2:3, :] = jnp.sum(low.astype(f32), 0, keepdims=True)
    outs[1][3:8, :] = jnp.zeros((5, total.shape[1]), f32)
    return low


def everyone_kernel(steps, value, out, sending, arriving, sems):
    partners = []
    for axis, stride in steps:
        at = lax.axis_index(axis)
        partners.append({axis: at + stride - 2 * stride * ((at // stride) % 2)})
    meet(partners)
    out[...] = value[...]
    for place, partner in enumerate(partners):
        sending[place] = out[...]
        send(sending.at[place], arriving.at[place], partner, sems, place).wait()
        out[...] = out[...] + arriving[place]


def everyone_call(number, sizes, value):
    steps = []
    for axis, size in zip(("fsdp", "ctx", "tp"), sizes):
        stride = 1
        while stride < size:
            steps.append((axis, stride))
            stride *= 2
    vmem = pl.BlockSpec(memory_space=pltpu.VMEM)
    held = pltpu.VMEM((len(steps),) + value.shape, f32)
    return pl.pallas_call(
        functools.partial(everyone_kernel, steps),
        out_shape=jax.ShapeDtypeStruct(value.shape, f32),
        in_specs=[vmem],
        out_specs=vmem,
        scratch_shapes=[held, held, pltpu.SemaphoreType.DMA((2, len(steps)))],
        compiler_params=pltpu.CompilerParams(
            collective_id=number, has_side_effects=True, vmem_limit_bytes=32 * 1024 * 1024
        ),
        name="sum_everywhere",
    )(value)


def local(
    sizes,
    tokens,
    counts,
    qkv_weight,
    qv_bias,
    out_weight,
    out_bias,
    norm_gain,
    norm_bias,
    up_weight,
    up_bias,
    down_weight,
    down_bias,
    cotangent,
):
    n_fsdp, n_ctx, n_tp = sizes
    swap = n_fsdp == n_tp
    head_axis, image_axis = ("fsdp", "tp") if swap else ("tp", "fsdp")
    n_head = n_tp
    pairs = [(f * n_tp + t, t * n_tp + f) for f in range(n_fsdp) for t in range(n_tp)]

    def exchange(value):
        return lax.ppermute(value, ("fsdp", "tp"), pairs) if swap else value

    capacity, width = tokens.shape[1:]
    layers = qkv_weight.shape[0]
    head_width = qkv_weight.shape[3]
    hidden_width = up_weight.shape[2]
    even = n_ctx == 2
    live = counts[0][lax.axis_index("ctx")]
    if even:
        rows = capacity * 4 // 5
        moved = capacity - rows
        kept = rows - moved
        is_full = live > rows
        other_pairs = [(0, 1), (1, 0)]
    else:
        rows = capacity
    share = rows // n_head

    use_kernels = swap and even and n_head == 4 and share % 16 == 0

    def other(value):
        return lax.ppermute(value, "ctx", other_pairs)

    def across(value, axis, stride):
        return lax.ppermute(value, axis, [(i, i ^ stride) for i in range(lax.axis_size(axis))])

    def bit_of(axis, stride):
        return (lax.axis_index(axis) // stride) % 2

    def doubled(value, axis, stride, dim):
        arrived = across(value, axis, stride)
        is_low = bit_of(axis, stride) == 0
        return jnp.concatenate(
            [jnp.where(is_low, value, arrived), jnp.where(is_low, arrived, value)], dim
        )

    def halved(value, axis, stride):
        bit = bit_of(axis, stride)
        leaving = lax.dynamic_index_in_dim(value, 1 - bit, 0, keepdims=False)
        staying = lax.dynamic_index_in_dim(value, bit, 0, keepdims=False)
        arrived = across(leaving, axis, stride)
        return (staying.astype(f32) + arrived.astype(f32)).astype(bf16)

    def gather_four(value, axis):
        return doubled(doubled(value, axis, 1, 0), axis, 2, 0)

    def gather_blocks(value):
        rows_here, columns = value.shape
        whole = gather_four(value[None, None], image_axis)
        return doubled(whole, "ctx", 1, 1).reshape(8 * rows_here, columns)

    def sum_blocks(value):
        columns = value.shape[1]
        value = value.reshape(4, 2, -1, columns)
        value = halved(jnp.transpose(value, (1, 0, 2, 3)), "ctx", 1)
        value = halved(value.reshape((2, 2) + value.shape[1:]), image_axis, 2)
        return halved(value, image_axis, 1)

    def packed(layer_no):
        return jnp.concatenate(
            [
                up_weight[layer_no],
                down_weight[layer_no].T,
                out_weight[layer_no].T,
                qkv_weight[layer_no, 0],
                qkv_weight[layer_no, 1],
                qkv_weight[layer_no, 2],
            ],
            1,
        )

    cuts = (0, hidden_width, 2 * hidden_width, 2 * hidden_width + head_width)

    def fetch(layer_no):
        mine = packed(layer_no)

        def spread(piece, pairwise):
            if pairwise and use_kernels:
                return gather_blocks(exchange(piece))
            return lax.all_gather(exchange(piece), (image_axis, "ctx"), axis=0, tiled=True)

        att, mlp = spread(mine[:, cuts[2] :], layer_no == 0), spread(mine[:, : cuts[2]], False)
        return (
            mlp[:, :hidden_width],
            mlp[:, hidden_width:],
            att[:, :head_width],
            att[:, head_width:],
        )

    weights = [fetch(layer_no) for layer_no in range(layers)]
    biases = exchange(jnp.concatenate([qv_bias.reshape(-1), up_bias.reshape(-1)]))
    qv_local = biases[: qv_bias.size].reshape(qv_bias.shape)
    up_local = biases[qv_bias.size :].reshape(up_bias.shape)

    both = jnp.stack([tokens[0], cotangent[0]])
    if even:
        arrived = other(both[:, rows:])
        both = jnp.concatenate(
            [both[:, :kept], jnp.where(is_full, both[:, kept:rows], arrived)], 1
        )
        usable = None
    else:
        both = both * (jnp.arange(capacity) < live).astype(bf16)[None, :, None]
        image_counts = exchange(counts[0])
        index = jnp.arange(capacity * n_ctx, dtype=jnp.int32)
        usable = (index % capacity < jnp.repeat(image_counts, capacity))[None, None, :]
    own_live = None
    if not even:
        place = jnp.arange(capacity, dtype=jnp.int32)
        own_live = (place < exchange(counts[0])[lax.axis_index("ctx")]).astype(f32)[:, None]
    start = lax.axis_index("tp") * share
    both = exchange(lax.dynamic_slice_in_dim(both, start, share, 1)).astype(f32)
    stream, grad = both[0], both[1]

    def gather(value):
        if use_kernels:
            return gather_four(value, head_axis)
        return lax.all_gather(value, head_axis, axis=0, tiled=True)

    def scatter(value):
        return lax.psum_scatter(
            value.astype(bf16), head_axis, scatter_dimension=0, tiled=True
        ).astype(f32)

    def constants(*entries):
        return jnp.pad(jnp.stack(entries), ((0, 8 - len(entries)), (0, 0)))

    wide, thin = (share, width), (share, 1)

    def forward_join(partial, base, bias, gain, shift):
        if use_kernels:
            return group_call(
                "sum_norm_gather", 0, head_axis, forward_middle, True, partial.astype(bf16),
                (base, constants(bias, gain, shift)), (wide, wide, thin),
            )
        total = base + scatter(partial) + bias
        normal_part, inverse = norm_parts(total)
        return total, normal_part, inverse, gather((normal_part * gain + shift).astype(bf16))

    def last_join(partial, base, bias, low):
        if use_kernels:
            return group_call(
                "sum_then_gather", 1, head_axis, last_middle, True, partial.astype(bf16),
                (base, constants(bias), low), (wide,),
            )
        return base + scatter(partial) + bias, gather(low)

    def backward_join(partial, base, normal_part, inverse, gain, last):
        if use_kernels:
            updated, sums, *low = group_call(
                "sum_norm_last" if last else "sum_norm_back", 3 if last else 2, head_axis,
                backward_middle, not last, partial.astype(bf16),
                (base, normal_part, inverse, constants(gain, gain)), (wide, (8, width)),
            )
            return updated, sums[0], sums[1], sums[2], (low[0] if low else None)
        change, gain_sum, shift_sum = norm_backward(scatter(partial), normal_part, inverse, gain)
        updated = base + change
        low = updated.astype(bf16)
        low_sum = jnp.sum(low.astype(f32), 0)
        return updated, gain_sum, shift_sum, low_sum, (None if last else gather(low))

    def everyone(value):
        if use_kernels:
            return everyone_call(4, sizes, value.reshape(-1, 128)).reshape(value.shape)
        return lax.psum(value, ("fsdp", "ctx", "tp"))

    def finish(value):
        value = exchange(value.astype(bf16))
        if use_kernels:
            whole = gather_four(value, "tp")
        else:
            whole = lax.all_gather(value, "tp", axis=0, tiled=True)
        if even:
            tail = whole[kept:]
            arrived = other(tail)
            nothing = jnp.zeros_like(tail)
            return jnp.concatenate(
                [
                    whole[:kept],
                    jnp.where(is_full, tail, nothing),
                    jnp.where(is_full, arrived, nothing),
                ],
                0,
            )[None]
        return (whole * (jnp.arange(capacity) < live).astype(bf16)[:, None])[None]

    saved = []
    part_a, inverse_a = norm_parts(stream)
    low_a = gather((part_a * norm_gain[0, 0] + norm_bias[0, 0]).astype(bf16))
    share_m = grad.astype(bf16)
    for layer_no in range(layers):
        up_full, down_full, out_full, qkv_full = weights[layer_no]
        shift = jnp.concatenate(
            [qv_local[layer_no, 0], jnp.zeros((head_width,), f32), qv_local[layer_no, 1]]
        )
        project = (dot(low_a, qkv_full, (1, 0)) + shift).astype(bf16)
        query, own_kv = project[:, :head_width], project[:, head_width:]
        if even:
            all_kv = jnp.concatenate([own_kv, other(own_kv)], 0)
        else:
            all_kv = lax.all_gather(own_kv, "ctx", axis=0, tiled=True)
        keys, values = all_kv[:, :head_width], all_kv[:, head_width:]
        attended, log_total = attention_forward(query, keys, values, usable)
        low_attended = attended.astype(bf16)
        hidden, part_c, inverse_c, low_c = forward_join(
            dot(low_attended, out_full, (1, 1)),
            stream,
            out_bias[layer_no],
            norm_gain[layer_no, 1],
            norm_bias[layer_no, 1],
        )
        pre_act = dot(low_c, up_full, (1, 0)) + up_local[layer_no]
        low_z = gelu_exact(pre_act).astype(bf16)
        saved.append(
            (part_a, inverse_a, low_a, query, keys, values, attended, log_total, low_attended)
            + (part_c, inverse_c, low_c, pre_act, low_z)
        )
        branch = dot(low_z, down_full, (1, 1))
        if layer_no + 1 < layers:
            stream, part_a, inverse_a, low_a = forward_join(
                branch,
                hidden,
                down_bias[layer_no],
                norm_gain[layer_no + 1, 0],
                norm_bias[layer_no + 1, 0],
            )
        else:
            stream, low_m = last_join(branch, hidden, down_bias[layer_no], share_m)
    block_output = finish(stream)

    def owned(value):
        if use_kernels:
            return exchange(sum_blocks(value)).astype(f32)
        return exchange(
            lax.psum_scatter(
                value.astype(bf16), (image_axis, "ctx"), scatter_dimension=0, tiled=True
            )
        ).astype(f32)

    outs = [None] * layers
    smalls = [None] * layers
    sum_m = jnp.sum(share_m.astype(f32), 0)
    head_place = lax.axis_index(head_axis)
    for layer_no in reversed(range(layers)):
        up_full, down_full, out_full, qkv_full = weights[layer_no]
        (part_a, inverse_a, low_a, query, keys, values, attended, log_total, low_attended) = saved[
            layer_no
        ][:9]
        part_c, inverse_c, low_c, pre_act, low_z = saved[layer_no][9:]
        grad_z = dot(low_m, down_full, (1, 0))
        _, gelu_pull = jax.vjp(gelu_exact, pre_act)
        low_dpre = gelu_pull(grad_z)[0].astype(bf16)
        if own_live is not None:
            low_dpre = low_dpre * own_live.astype(bf16)
        partial_c = dot(low_dpre, up_full, (1, 1)).astype(bf16)
        mlp_grads = jnp.concatenate(
            [dot(low_c, low_dpre, (0, 0)), dot(low_m, low_z, (0, 0))], 1
        ).astype(bf16)
        partial_c, mlp_grads = lax.optimization_barrier((partial_c, mlp_grads))
        mlp_owned = owned(mlp_grads)
        grad_h, gain_two, shift_two, sum_mix, low_mix = backward_join(
            partial_c, grad, part_c, inverse_c, norm_gain[layer_no, 1], False
        )
        grad_attended = dot(low_mix, out_full, (1, 0)).astype(bf16)
        grad_query, grad_keys, grad_values = attention_backward(
            query, keys, values, grad_attended, attended, log_total, usable
        )
        grad_kv = jnp.concatenate([grad_keys, grad_values], 1)
        if even:
            grad_kv = (grad_kv[:rows].astype(f32) + other(grad_kv[rows:]).astype(f32)).astype(bf16)
        else:
            grad_kv = lax.psum_scatter(grad_kv, "ctx", scatter_dimension=0, tiled=True)
        stacked = jnp.concatenate([grad_query, grad_kv], 1)
        partial_a = dot(stacked, qkv_full, (1, 1)).astype(bf16)
        att_grads = jnp.concatenate(
            [dot(low_mix, low_attended, (0, 0)), dot(low_a, stacked, (0, 0))], 1
        ).astype(bf16)
        partial_a, att_grads = lax.optimization_barrier((partial_a, att_grads))
        att_owned = owned(att_grads)
        sum_m_here = sum_m
        grad, gain_one, shift_one, sum_m, low_m = backward_join(
            partial_a, grad_h, part_a, inverse_a, norm_gain[layer_no, 0], layer_no == 0
        )
        qkv_sums = jnp.sum(stacked.astype(f32), 0)
        placed = jnp.concatenate(
            [
                qkv_sums[:head_width],
                qkv_sums[2 * head_width :],
                jnp.sum(low_dpre.astype(f32), 0),
            ]
        )
        slots = jnp.where(jnp.arange(n_head)[:, None] == head_place, placed[None], 0.0)
        smalls[layer_no] = jnp.concatenate(
            [gain_one, gain_two, shift_one, shift_two, sum_mix, sum_m_here, slots.reshape(-1)]
        )
        outs[layer_no] = (
            jnp.transpose(
                att_owned[:, head_width:].reshape(att_owned.shape[0], 3, head_width), (1, 0, 2)
            ),
            att_owned[:, :head_width].T,
            mlp_owned[:, :hidden_width],
            mlp_owned[:, hidden_width:].T,
        )
    grad_tokens = finish(grad).astype(f32)
    summed = everyone(jnp.stack(smalls))
    shared = summed[:, : 6 * width].reshape(layers, 6, width)
    mine = lax.dynamic_index_in_dim(
        summed[:, 6 * width :].reshape(layers, n_head, -1), lax.axis_index("tp"), 1, keepdims=False
    )
    grad_qkv, grad_out, grad_up, grad_down = (jnp.stack(entry) for entry in zip(*outs))
    return (
        block_output,
        grad_tokens,
        grad_qkv,
        mine[:, : 2 * head_width].reshape(layers, 2, head_width),
        grad_out,
        shared[:, 4],
        shared[:, 0:2],
        shared[:, 2:4],
        grad_up,
        mine[:, 2 * head_width :],
        grad_down,
        shared[:, 5],
    )


def solution(mesh):
    sizes = tuple(mesh.shape[name] for name in ("fsdp", "ctx", "tp"))
    return jax.shard_map(
        functools.partial(local, sizes),
        mesh=mesh,
        in_specs=(
            P("fsdp", "ctx", None),
            P("fsdp", None),
            P(None, None, ("fsdp", "ctx"), "tp"),
            P(None, None, "tp"),
            P(None, "tp", ("fsdp", "ctx")),
            P(),
            P(),
            P(),
            P(None, ("fsdp", "ctx"), "tp"),
            P(None, "tp"),
            P(None, "tp", ("fsdp", "ctx")),
            P(),
            P("fsdp", "ctx", None),
        ),
        out_specs=(
            P("fsdp", "ctx", None),
            P("fsdp", "ctx", None),
            P(None, None, ("fsdp", "ctx"), "tp"),
            P(None, None, "tp"),
            P(None, "tp", ("fsdp", "ctx")),
            P(),
            P(),
            P(),
            P(None, ("fsdp", "ctx"), "tp"),
            P(None, "tp"),
            P(None, "tp", ("fsdp", "ctx")),
            P(),
        ),
        check_vma=False,
    )
```

```python
import functools

import jax
import jax.numpy as jnp
from jax import lax
from jax.experimental import pallas as pl
from jax.experimental.pallas import tpu as pltpu
from jax.sharding import PartitionSpec as P

HD = 64
norm_eps = 1e-06
big_negative = -1e30
f32 = jnp.float32
bf16 = jnp.bfloat16


def norm_parts(values):
    centred = values - jnp.mean(values, -1, keepdims=True)
    inverse = lax.rsqrt(jnp.mean(centred * centred, -1, keepdims=True) + norm_eps)
    return centred * inverse, inverse


def norm_backward(grad_out, normal_part, inverse, norm_scale):
    scaled = grad_out * norm_scale
    inner = (
        scaled
        - jnp.mean(scaled, -1, keepdims=True)
        - normal_part * jnp.mean(scaled * normal_part, -1, keepdims=True)
    )
    return (inner * inverse, jnp.sum(grad_out * normal_part, 0), jnp.sum(grad_out, 0))


def gelu_exact(pre_act):
    return jax.nn.gelu(pre_act, approximate=False)


def dot(a, b, contract):
    return lax.dot_general(a, b, ((contract[0:1], contract[1:2]), ((), ())), preferred_element_type=f32)


def split_heads(values):
    return values.reshape(values.shape[0], values.shape[1] // HD, HD)


def attention_forward(query, keys, values, usable):
    rows, width = query.shape
    scores = (
        jnp.einsum("qhd,khd->hqk", split_heads(query), split_heads(keys), preferred_element_type=f32)
        * HD ** (-0.5)
    )
    if usable is not None:
        scores = jnp.where(usable, scores, big_negative)
    top = jnp.max(scores, -1, keepdims=True)
    weights = jnp.exp(scores - top)
    total = jnp.sum(weights, -1, keepdims=True)
    accum = jnp.einsum(
        "hqk,khd->hqd", weights.astype(bf16), split_heads(values), preferred_element_type=f32
    )
    attended = accum / total
    return jnp.transpose(attended, (1, 0, 2)).reshape(rows, width), top + jnp.log(total)


def attention_backward(query, keys, values, grad_attended, attended, log_total, usable):
    rows, width = query.shape
    scale = HD ** (-0.5)
    query_heads, key_heads, value_heads = split_heads(query), split_heads(keys), split_heads(values)
    grad_heads = split_heads(grad_attended)
    delta = jnp.transpose(jnp.sum(grad_heads.astype(f32) * split_heads(attended), -1))[..., None]
    scores = jnp.einsum("qhd,khd->hqk", query_heads, key_heads, preferred_element_type=f32) * scale
    if usable is not None:
        scores = jnp.where(usable, scores, big_negative)
    probs = jnp.exp(scores - log_total)
    grad_probs = jnp.einsum("qhd,khd->hqk", grad_heads, value_heads, preferred_element_type=f32)
    grad_scores = (probs * (grad_probs - delta)).astype(bf16)
    grad_query = (
        jnp.einsum("hqk,khd->qhd", grad_scores, key_heads, preferred_element_type=f32) * scale
    )
    grad_keys = (
        jnp.einsum("hqk,qhd->khd", grad_scores, query_heads, preferred_element_type=f32) * scale
    )
    grad_values = jnp.einsum(
        "hqk,qhd->khd", probs.astype(bf16), grad_heads, preferred_element_type=f32
    )
    length = keys.shape[0]
    return (
        grad_query.reshape(rows, width).astype(bf16),
        grad_keys.reshape(length, width).astype(bf16),
        grad_values.reshape(length, width).astype(bf16),
    )


MESH = pl.DeviceIdType.MESH


def meet(partners):
    barrier = pltpu.get_barrier_semaphore()
    for partner in partners:
        pl.semaphore_signal(barrier, inc=1, device_id=partner, device_id_type=MESH)
    pl.semaphore_wait(barrier, len(partners))


def send(source, target, partner, sems, place):
    copy = pltpu.make_async_remote_copy(
        src_ref=source,
        dst_ref=target,
        send_sem=sems.at[0, place],
        recv_sem=sems.at[1, place],
        device_id=partner,
        device_id_type=MESH,
    )
    copy.start()
    return copy


def group_kernel(axis, middle, with_gather, n_in, n_out, partial, *refs):
    ins, outs = refs[:n_in], refs[n_in : n_in + n_out]
    scratch = refs[n_in + n_out :]
    near_recv, far_send, far_recv, near_sems, far_sem = scratch[:5]
    me = lax.axis_index(axis)
    near_at, far_at = me + 1 - 2 * (me % 2), (me + 2) % 4
    cross_at = (near_at + 2) % 4
    near, far = {axis: near_at}, {axis: far_at}
    share = near_recv.shape[1]
    meet((near, far))

    def rows_of(place):
        return pl.ds(pl.multiple_of(place * share, share), share)

    first = send(partial.at[rows_of(cross_at)], near_recv.at[0], near, near_sems, 0)
    second = send(partial.at[rows_of(near_at)], near_recv.at[1], near, near_sems, 1)
    first.wait()
    far_send[...] = (
        partial[rows_of(far_at), :].astype(f32) + near_recv[0].astype(f32)
    ).astype(bf16)
    across = send(far_send, far_recv, far, far_sem, 0)
    second.wait()
    across.wait()
    total = (
        partial[rows_of(me), :].astype(f32)
        + near_recv[1].astype(f32)
        + far_recv[...].astype(f32)
    )
    low = middle(total, ins, outs)
    if not with_gather:
        return
    whole, gather_sems = scratch[5:]
    whole[me] = low
    over = send(whole.at[me], whole.at[me], far, gather_sems, 0)
    beside = send(whole.at[me], whole.at[me], near, gather_sems, 1)
    over.wait()
    onward = send(whole.at[far_at], whole.at[far_at], near, gather_sems, 2)
    beside.wait()
    onward.wait()
    for place in range(4):
        outs[-1][place * share : (place + 1) * share, :] = whole[place]


def group_call(name, number, axis, middle, with_gather, partial, ins, outs):
    rows, width = partial.shape
    share = rows // 4
    shapes = [jax.ShapeDtypeStruct(shape, f32) for shape in outs]
    if with_gather:
        shapes.append(jax.ShapeDtypeStruct((rows, width), bf16))
    scratch = [
        pltpu.VMEM((2, share, width), bf16),
        pltpu.VMEM((share, width), bf16),
        pltpu.VMEM((share, width), bf16),
        pltpu.SemaphoreType.DMA((2, 2)),
        pltpu.SemaphoreType.DMA((2, 1)),
    ]
    if with_gather:
        scratch += [pltpu.VMEM((4, share, width), bf16), pltpu.SemaphoreType.DMA((2, 3))]
    vmem = pl.BlockSpec(memory_space=pltpu.VMEM)
    return pl.pallas_call(
        functools.partial(group_kernel, axis, middle, with_gather, len(ins), len(shapes)),
        out_shape=shapes,
        in_specs=[vmem] * (1 + len(ins)),
        out_specs=[vmem] * len(shapes),
        scratch_shapes=scratch,
        compiler_params=pltpu.CompilerParams(
            collective_id=number, has_side_effects=True, vmem_limit_bytes=32 * 1024 * 1024
        ),
        cost_estimate=pl.CostEstimate(
            flops=rows * width * 10, bytes_accessed=rows * width * 8, transcendentals=0
        ),
        name=name,
    )(partial, *ins)


def forward_middle(total, ins, outs):
    stream, consts = ins
    hidden = stream[...] + total + consts[0:1, :]
    normal_part, inverse = norm_parts(hidden)
    outs[0][...] = hidden
    outs[1][...] = normal_part
    outs[2][...] = inverse
    return (normal_part * consts[1:2, :] + consts[2:3, :]).astype(bf16)


def last_middle(total, ins, outs):
    stream, consts, low = ins
    outs[0][...] = stream[...] + total + consts[0:1, :]
    return low[...]


def backward_middle(total, ins, outs):
    grad, normal_part, inverse, consts = ins
    part = normal_part[...]
    scaled = total * consts[1:2, :]
    inner = (
        scaled
        - jnp.mean(scaled, -1, keepdims=True)
        - part * jnp.mean(scaled * part, -1, keepdims=True)
    )
    updated = grad[...] + inner * inverse[...]
    low = updated.astype(bf16)
    outs[0][...] = updated
    outs[1][0:1, :] = jnp.sum(total * part, 0, keepdims=True)
    outs[1][1:2, :] = jnp.sum(total, 0, keepdims=True)
    outs[1][2:3, :] = jnp.sum(low.astype(f32), 0, keepdims=True)
    outs[1][3:8, :] = jnp.zeros((5, total.shape[1]), f32)
    return low


def everyone_kernel(steps, value, out, sending, arriving, sems):
    partners = []
    for axis, stride in steps:
        at = lax.axis_index(axis)
        partners.append({axis: at + stride - 2 * stride * ((at // stride) % 2)})
    meet(partners)
    out[...] = value[...]
    for place, partner in enumerate(partners):
        sending[place] = out[...]
        send(sending.at[place], arriving.at[place], partner, sems, place).wait()
        out[...] = out[...] + arriving[place]


def everyone_call(number, sizes, value):
    steps = []
    for axis, size in zip(("fsdp", "ctx", "tp"), sizes):
        stride = 1
        while stride < size:
            steps.append((axis, stride))
            stride *= 2
    vmem = pl.BlockSpec(memory_space=pltpu.VMEM)
    held = pltpu.VMEM((len(steps),) + value.shape, f32)
    return pl.pallas_call(
        functools.partial(everyone_kernel, steps),
        out_shape=jax.ShapeDtypeStruct(value.shape, f32),
        in_specs=[vmem],
        out_specs=vmem,
        scratch_shapes=[held, held, pltpu.SemaphoreType.DMA((2, len(steps)))],
        compiler_params=pltpu.CompilerParams(
            collective_id=number, has_side_effects=True, vmem_limit_bytes=32 * 1024 * 1024
        ),
        name="sum_everywhere",
    )(value)


def local(
    sizes,
    tokens,
    counts,
    qkv_weight,
    qv_bias,
    out_weight,
    out_bias,
    norm_gain,
    norm_bias,
    up_weight,
    up_bias,
    down_weight,
    down_bias,
    cotangent,
):
    n_fsdp, n_ctx, n_tp = sizes
    swap = n_fsdp == n_tp
    head_axis, image_axis = ("fsdp", "tp") if swap else ("tp", "fsdp")
    n_head = n_tp
    pairs = [(f * n_tp + t, t * n_tp + f) for f in range(n_fsdp) for t in range(n_tp)]

    def exchange(value):
        return lax.ppermute(value, ("fsdp", "tp"), pairs) if swap else value

    capacity, width = tokens.shape[1:]
    layers = qkv_weight.shape[0]
    head_width = qkv_weight.shape[3]
    hidden_width = up_weight.shape[2]
    even = n_ctx == 2
    live = counts[0][lax.axis_index("ctx")]
    if even:
        rows = capacity * 4 // 5
        moved = capacity - rows
        kept = rows - moved
        is_full = live > rows
        other_pairs = [(0, 1), (1, 0)]
    else:
        rows = capacity
    share = rows // n_head

    use_kernels = swap and even and n_head == 4 and share % 16 == 0

    def other(value):
        return lax.ppermute(value, "ctx", other_pairs)

    def across(value, axis, stride):
        return lax.ppermute(value, axis, [(i, i ^ stride) for i in range(lax.axis_size(axis))])

    def bit_of(axis, stride):
        return (lax.axis_index(axis) // stride) % 2

    def doubled(value, axis, stride, dim):
        arrived = across(value, axis, stride)
        is_low = bit_of(axis, stride) == 0
        return jnp.concatenate(
            [jnp.where(is_low, value, arrived), jnp.where(is_low, arrived, value)], dim
        )

    def halved(value, axis, stride):
        bit = bit_of(axis, stride)
        leaving = lax.dynamic_index_in_dim(value, 1 - bit, 0, keepdims=False)
        staying = lax.dynamic_index_in_dim(value, bit, 0, keepdims=False)
        arrived = across(leaving, axis, stride)
        return (staying.astype(f32) + arrived.astype(f32)).astype(bf16)

    def gather_four(value, axis):
        return doubled(doubled(value, axis, 1, 0), axis, 2, 0)

    def gather_blocks(value):
        rows_here, columns = value.shape
        whole = gather_four(value[None, None], image_axis)
        return doubled(whole, "ctx", 1, 1).reshape(8 * rows_here, columns)

    def first_step(value):
        value = value.reshape(4, 2, -1, value.shape[1])
        value = halved(jnp.transpose(value, (1, 0, 2, 3)), "ctx", 1)
        return value.reshape((2, 2) + value.shape[1:])

    sum_steps = (
        first_step,
        lambda value: halved(value, image_axis, 2),
        lambda value: halved(value, image_axis, 1),
        exchange,
    )
    chains = []

    def advance(tie, grads=None):
        moving = [chain for chain in chains if chain[1] < len(sum_steps)]
        done = [sum_steps[chain[1]](chain[0]) for chain in moving]
        tie, grads, done = lax.optimization_barrier((tie, grads, done))
        for chain, value in zip(moving, done):
            chain[0] = value
            chain[1] += 1
        if grads is not None:
            chains.append([grads, 0])
        return tie

    def packed(layer_no):
        return jnp.concatenate(
            [
                up_weight[layer_no],
                down_weight[layer_no].T,
                out_weight[layer_no].T,
                qkv_weight[layer_no, 0],
                qkv_weight[layer_no, 1],
                qkv_weight[layer_no, 2],
            ],
            1,
        )

    cuts = (0, hidden_width, 2 * hidden_width, 2 * hidden_width + head_width)

    first_weights = []

    def spread(piece):
        piece = exchange(piece)
        if use_kernels and not first_weights:
            first_weights.append(gather_blocks(piece))
            return first_weights[0]
        if use_kernels:
            piece = lax.optimization_barrier((piece, first_weights[0]))[0]
        return lax.all_gather(piece, (image_axis, "ctx"), axis=0, tiled=True)

    def fetch(layer_no):
        mine = packed(layer_no)
        att, mlp = spread(mine[:, cuts[2] :]), spread(mine[:, : cuts[2]])
        return (
            mlp[:, :hidden_width],
            mlp[:, hidden_width:],
            att[:, :head_width],
            att[:, head_width:],
        )

    weights = [fetch(layer_no) for layer_no in range(layers)]
    biases = exchange(jnp.concatenate([qv_bias.reshape(-1), up_bias.reshape(-1)]))
    qv_local = biases[: qv_bias.size].reshape(qv_bias.shape)
    up_local = biases[qv_bias.size :].reshape(up_bias.shape)

    both = jnp.stack([tokens[0], cotangent[0]])
    if even:
        arrived = other(both[:, rows:])
        both = jnp.concatenate(
            [both[:, :kept], jnp.where(is_full, both[:, kept:rows], arrived)], 1
        )
        usable = None
    else:
        both = both * (jnp.arange(capacity) < live).astype(bf16)[None, :, None]
        image_counts = exchange(counts[0])
        index = jnp.arange(capacity * n_ctx, dtype=jnp.int32)
        usable = (index % capacity < jnp.repeat(image_counts, capacity))[None, None, :]
    own_live = None
    if not even:
        place = jnp.arange(capacity, dtype=jnp.int32)
        own_live = (place < exchange(counts[0])[lax.axis_index("ctx")]).astype(f32)[:, None]
    start = lax.axis_index("tp") * share
    both = exchange(lax.dynamic_slice_in_dim(both, start, share, 1)).astype(f32)
    stream, grad = both[0], both[1]

    def gather(value):
        if use_kernels:
            return gather_four(value, head_axis)
        return lax.all_gather(value, head_axis, axis=0, tiled=True)

    def scatter(value):
        return lax.psum_scatter(
            value.astype(bf16), head_axis, scatter_dimension=0, tiled=True
        ).astype(f32)

    def constants(*entries):
        return jnp.pad(jnp.stack(entries), ((0, 8 - len(entries)), (0, 0)))

    wide, thin = (share, width), (share, 1)

    def forward_join(partial, base, bias, gain, shift):
        if use_kernels:
            return group_call(
                "sum_norm_gather", 0, head_axis, forward_middle, True, partial.astype(bf16),
                (base, constants(bias, gain, shift)), (wide, wide, thin),
            )
        total = base + scatter(partial) + bias
        normal_part, inverse = norm_parts(total)
        return total, normal_part, inverse, gather((normal_part * gain + shift).astype(bf16))

    def last_join(partial, base, bias, low):
        if use_kernels:
            return group_call(
                "sum_then_gather", 1, head_axis, last_middle, True, partial.astype(bf16),
                (base, constants(bias), low), (wide,),
            )
        return base + scatter(partial) + bias, gather(low)

    def backward_join(partial, base, normal_part, inverse, gain, last):
        if use_kernels:
            updated, sums, *low = group_call(
                "sum_norm_last" if last else "sum_norm_back", 3 if last else 2, head_axis,
                backward_middle, not last, partial.astype(bf16),
                (base, normal_part, inverse, constants(gain, gain)), (wide, (8, width)),
            )
            return updated, sums[0], sums[1], sums[2], (low[0] if low else None)
        change, gain_sum, shift_sum = norm_backward(scatter(partial), normal_part, inverse, gain)
        updated = base + change
        low = updated.astype(bf16)
        low_sum = jnp.sum(low.astype(f32), 0)
        return updated, gain_sum, shift_sum, low_sum, (None if last else gather(low))

    def everyone(value):
        if use_kernels:
            return everyone_call(4, sizes, value.reshape(-1, 128)).reshape(value.shape)
        return lax.psum(value, ("fsdp", "ctx", "tp"))

    def finish(value):
        value = exchange(value.astype(bf16))
        if use_kernels:
            whole = gather_four(value, "tp")
        else:
            whole = lax.all_gather(value, "tp", axis=0, tiled=True)
        if even:
            tail = whole[kept:]
            arrived = other(tail)
            nothing = jnp.zeros_like(tail)
            return jnp.concatenate(
                [
                    whole[:kept],
                    jnp.where(is_full, tail, nothing),
                    jnp.where(is_full, arrived, nothing),
                ],
                0,
            )[None]
        return (whole * (jnp.arange(capacity) < live).astype(bf16)[:, None])[None]

    saved = []
    part_a, inverse_a = norm_parts(stream)
    low_a = gather((part_a * norm_gain[0, 0] + norm_bias[0, 0]).astype(bf16))
    share_m = grad.astype(bf16)
    for layer_no in range(layers):
        up_full, down_full, out_full, qkv_full = weights[layer_no]
        shift = jnp.concatenate(
            [qv_local[layer_no, 0], jnp.zeros((head_width,), f32), qv_local[layer_no, 1]]
        )
        project = (dot(low_a, qkv_full, (1, 0)) + shift).astype(bf16)
        query, own_kv = project[:, :head_width], project[:, head_width:]
        if even:
            all_kv = jnp.concatenate([own_kv, other(own_kv)], 0)
        else:
            all_kv = lax.all_gather(own_kv, "ctx", axis=0, tiled=True)
        keys, values = all_kv[:, :head_width], all_kv[:, head_width:]
        attended, log_total = attention_forward(query, keys, values, usable)
        low_attended = attended.astype(bf16)
        hidden, part_c, inverse_c, low_c = forward_join(
            dot(low_attended, out_full, (1, 1)),
            stream,
            out_bias[layer_no],
            norm_gain[layer_no, 1],
            norm_bias[layer_no, 1],
        )
        pre_act = dot(low_c, up_full, (1, 0)) + up_local[layer_no]
        low_z = gelu_exact(pre_act).astype(bf16)
        saved.append(
            (part_a, inverse_a, low_a, query, keys, values, attended, log_total, low_attended)
            + (part_c, inverse_c, low_c, pre_act, low_z)
        )
        branch = dot(low_z, down_full, (1, 1))
        if layer_no + 1 < layers:
            stream, part_a, inverse_a, low_a = forward_join(
                branch,
                hidden,
                down_bias[layer_no],
                norm_gain[layer_no + 1, 0],
                norm_bias[layer_no + 1, 0],
            )
        else:
            stream, low_m = last_join(branch, hidden, down_bias[layer_no], share_m)
    block_output = finish(stream)

    def owned(value):
        return exchange(
            lax.psum_scatter(
                value.astype(bf16), (image_axis, "ctx"), scatter_dimension=0, tiled=True
            )
        ).astype(f32)

    outs = [None] * layers
    smalls = [None] * layers
    sum_m = jnp.sum(share_m.astype(f32), 0)
    head_place = lax.axis_index(head_axis)
    for layer_no in reversed(range(layers)):
        up_full, down_full, out_full, qkv_full = weights[layer_no]
        (part_a, inverse_a, low_a, query, keys, values, attended, log_total, low_attended) = saved[
            layer_no
        ][:9]
        part_c, inverse_c, low_c, pre_act, low_z = saved[layer_no][9:]
        grad_z = dot(low_m, down_full, (1, 0))
        _, gelu_pull = jax.vjp(gelu_exact, pre_act)
        low_dpre = gelu_pull(grad_z)[0].astype(bf16)
        if own_live is not None:
            low_dpre = low_dpre * own_live.astype(bf16)
        partial_c = dot(low_dpre, up_full, (1, 1)).astype(bf16)
        mlp_grads = jnp.concatenate(
            [dot(low_c, low_dpre, (0, 0)), dot(low_m, low_z, (0, 0))], 1
        ).astype(bf16)
        if use_kernels:
            partial_c = advance(partial_c, mlp_grads)
        else:
            outs[layer_no] = [owned(mlp_grads)]
        grad_h, gain_two, shift_two, sum_mix, low_mix = backward_join(
            partial_c, grad, part_c, inverse_c, norm_gain[layer_no, 1], False
        )
        grad_attended = dot(low_mix, out_full, (1, 0)).astype(bf16)
        grad_query, grad_keys, grad_values = attention_backward(
            query, keys, values, grad_attended, attended, log_total, usable
        )
        grad_kv = jnp.concatenate([grad_keys, grad_values], 1)
        if even:
            grad_kv = (grad_kv[:rows].astype(f32) + other(grad_kv[rows:]).astype(f32)).astype(bf16)
        else:
            grad_kv = lax.psum_scatter(grad_kv, "ctx", scatter_dimension=0, tiled=True)
        stacked = jnp.concatenate([grad_query, grad_kv], 1)
        partial_a = dot(stacked, qkv_full, (1, 1)).astype(bf16)
        att_grads = jnp.concatenate(
            [dot(low_mix, low_attended, (0, 0)), dot(low_a, stacked, (0, 0))], 1
        ).astype(bf16)
        if use_kernels:
            partial_a = advance(partial_a, att_grads)
        else:
            outs[layer_no].append(owned(att_grads))
        sum_m_here = sum_m
        grad, gain_one, shift_one, sum_m, low_m = backward_join(
            partial_a, grad_h, part_a, inverse_a, norm_gain[layer_no, 0], layer_no == 0
        )
        qkv_sums = jnp.sum(stacked.astype(f32), 0)
        placed = jnp.concatenate(
            [
                qkv_sums[:head_width],
                qkv_sums[2 * head_width :],
                jnp.sum(low_dpre.astype(f32), 0),
            ]
        )
        slots = jnp.where(jnp.arange(n_head)[:, None] == head_place, placed[None], 0.0)
        smalls[layer_no] = jnp.concatenate(
            [gain_one, gain_two, shift_one, shift_two, sum_mix, sum_m_here, slots.reshape(-1)]
        )
    if use_kernels:
        smalls = advance(smalls)
    grad_tokens = finish(grad).astype(f32)
    summed = everyone(jnp.stack(smalls))
    shared = summed[:, : 6 * width].reshape(layers, 6, width)
    mine = lax.dynamic_index_in_dim(
        summed[:, 6 * width :].reshape(layers, n_head, -1), lax.axis_index("tp"), 1, keepdims=False
    )
    if use_kernels:
        for chain in chains:
            for step in sum_steps[chain[1] :]:
                chain[0] = step(chain[0])
        owned_here = [chain[0].astype(f32) for chain in chains]
        for order, layer_no in enumerate(reversed(range(layers))):
            outs[layer_no] = owned_here[2 * order : 2 * order + 2]
    mlp_owned = jnp.stack([entry[0] for entry in outs])
    att_owned = jnp.stack([entry[1] for entry in outs])
    grad_out = jnp.swapaxes(att_owned[:, :, :head_width], 1, 2)
    grad_qkv = jnp.transpose(
        att_owned[:, :, head_width:].reshape(layers, -1, 3, head_width), (0, 2, 1, 3)
    )
    grad_up = mlp_owned[:, :, :hidden_width]
    grad_down = jnp.swapaxes(mlp_owned[:, :, hidden_width:], 1, 2)
    return (
        block_output,
        grad_tokens,
        grad_qkv,
        mine[:, : 2 * head_width].reshape(layers, 2, head_width),
        grad_out,
        shared[:, 4],
        shared[:, 0:2],
        shared[:, 2:4],
        grad_up,
        mine[:, 2 * head_width :],
        grad_down,
        shared[:, 5],
    )


def solution(mesh):
    sizes = tuple(mesh.shape[name] for name in ("fsdp", "ctx", "tp"))
    return jax.shard_map(
        functools.partial(local, sizes),
        mesh=mesh,
        in_specs=(
            P("fsdp", "ctx", None),
            P("fsdp", None),
            P(None, None, ("fsdp", "ctx"), "tp"),
            P(None, None, "tp"),
            P(None, "tp", ("fsdp", "ctx")),
            P(),
            P(),
            P(),
            P(None, ("fsdp", "ctx"), "tp"),
            P(None, "tp"),
            P(None, "tp", ("fsdp", "ctx")),
            P(),
            P("fsdp", "ctx", None),
        ),
        out_specs=(
            P("fsdp", "ctx", None),
            P("fsdp", "ctx", None),
            P(None, None, ("fsdp", "ctx"), "tp"),
            P(None, None, "tp"),
            P(None, "tp", ("fsdp", "ctx")),
            P(),
            P(),
            P(),
            P(None, ("fsdp", "ctx"), "tp"),
            P(None, "tp"),
            P(None, "tp", ("fsdp", "ctx")),
            P(),
        ),
        check_vma=False,
    )
```
